32 devices in a mesh: vox: 4 (over y, core), filt: 8 (over z, x).
Axes of the slice: x: 2, y: 2, z: 4, core: 2. Of those that a mesh axis runs over, the one named last changes fastest.
Arguments:
- volume: bfloat16 [1024, 16, 128], P('filt', 'vox'), may hold values from -6 to 6
- kernel: bfloat16 [27, 1024, 1024], P(None, 'filt', 'vox'), may hold values from -0.0390625 to 0.0390625
- bias: float32 [1024], P('filt'), may hold values from -3 to 3
Outputs:
- features: bfloat16 [1024, 16, 128], P('filt', 'vox')
The draws below stay inside these ranges and needn't reach their ends.
All inputs are finite; a program needn't handle non-finite values.
Results may differ from the reference program's by a relative error of at most 0.001.
Values may be sent and summed in bfloat16 or wider, within the bound.
A program may use at most 64 MiB of HBM per device.

```python
import jax
import jax.numpy as jnp
from jax import lax

C_IN = 1024
C_OUT = 1024
H = 4
W = 32
DEPTH = 16


def level_of(key, shape, pieces, least, high):
    gain, own = 1.0, jax.random.fold_in(key, 6)
    for position, blocks in pieces:
        heights = jnp.exp(jax.random.uniform(jax.random.fold_in(own, position), (blocks,), jnp.float32, least / len(pieces), high / len(pieces)))
        gain = gain * jnp.repeat(heights, shape[position] // blocks).reshape([-1 if axis == position else 1 for axis in range(len(shape))])
    return gain


def centred(key, shape, scale, limit, pieces=(), dtype=jnp.bfloat16):
    values = jax.random.normal(key, shape, jnp.float32) * scale
    if len(pieces) > 0:
        values = level_of(key, shape, pieces, -0.22, 0.18) * values
    return jnp.clip(values, min=-limit, max=limit).astype(dtype)


def setup_inputs(seed: int = 0) -> dict:
    key_list = jax.random.split(jax.random.key(seed), 4)
    volume = centred(key_list[0], (C_IN, DEPTH, H * W), 1.0, 6.0, ((0, 8), (1, 4)))
    kernel = centred(key_list[1], (27, C_OUT, C_IN), (27 * C_IN) ** -0.5, 0.0390625, ((1, 8), (2, 4)))
    bias = centred(key_list[2], (C_OUT,), 0.5, 3.0, ((0, 8),), jnp.float32)
    return dict(volume=volume, kernel=kernel, bias=bias)


def reference(volume, kernel, bias):
    channels = volume.shape[0]
    depth_all = volume.shape[1]
    filters = kernel.shape[1]
    volume_wide = volume.astype(jnp.float32).reshape(1, channels, depth_all, H, W)
    kernel_wide = kernel.astype(jnp.float32).reshape(3, 3, 3, filters, channels)
    summed = lax.conv_general_dilated(volume_wide, kernel_wide, (1, 1, 1), [(1, 1), (1, 1), (1, 1)], dimension_numbers=("NCDHW", "DHWOI", "NCDHW"), precision=lax.Precision.HIGHEST)
    result = summed[0] + bias[:, None, None, None]
    return result.reshape(filters, depth_all, H * W).astype(jnp.bfloat16)
```

```python
import functools

import jax
import jax.numpy as jnp
from jax import lax
from jax.experimental import pallas as pl
from jax.experimental.pallas import tpu as pltpu
from jax.sharding import PartitionSpec as P

H = 4
W = 32
MESH = pl.DeviceIdType.MESH


def body(
    nv, rep, vol, ker, out, held, slab, taps, prod, mine, away, near, far,
    tap_sem, own_sem, s1, r1, s2, r2, s3, r3, s4, r4, s5, r5,
):
    v = lax.axis_index("vox")
    f = lax.axis_index("filt")
    q = lax.div(f, rep)
    s = lax.rem(f, rep)
    planes, chans, cells = vol.shape
    filters = taps.shape[2]
    depth = taps.shape[3]
    half = nv // 2
    pair = lax.div(v, 2)
    core = lax.rem(v, 2)
    sibling = v + 1 - 2 * core

    load = pltpu.make_async_copy(ker, taps, tap_sem)
    load.start()

    barrier = pltpu.get_barrier_semaphore()
    peers = []
    for k in range(1, nv):
        peers.append((v, lax.rem(q + k, nv) * rep + s))
        peers.append((lax.rem(v + k, nv), f))
    for t in range(1, rep):
        peers.append((v, q * rep + lax.rem(s + t, rep)))
    for peer in peers:
        pl.semaphore_signal(barrier, inc=1, device_id=peer, device_id_type=MESH)
    pl.semaphore_wait(barrier, len(peers))

    def spot(owner, part):
        rows = pl.ds(pl.multiple_of(part * chans, chans), chans)
        return slab.at[pl.ds(1 + owner * planes, planes), rows, :]

    def gather_copy(k):
        return pltpu.make_async_remote_copy(
            vol, held.at[k], s1.at[k], r1.at[k],
            device_id=(v, lax.rem(q + k, nv) * rep + s), device_id_type=MESH)

    def cross_copy(src, k, target):
        return pltpu.make_async_remote_copy(
            src, spot(v, s), s2.at[k], r2.at[lax.rem(v - target + nv, nv)],
            device_id=(target, f), device_id_type=MESH)

    def side_copy(src, owner, j, t):
        return pltpu.make_async_remote_copy(
            src, spot(owner, s), s3.at[t, j], r3.at[t, j],
            device_id=(v, q * rep + lax.rem(s + t, rep)), device_id_type=MESH)

    def pass_on(k):
        origin = lax.rem(q - k + nv, nv)
        src = vol if k == 0 else held.at[k]

        @pl.when(origin == v)
        def _():
            for t in range(1, rep):
                side_copy(src, v, 0, t).start()
            pltpu.make_async_copy(src, spot(v, s), own_sem).start()

        @pl.when(origin != v)
        def _():
            cross_copy(src, k, origin).start()

    for k in range(1, nv):
        gather_copy(k).start()
    pass_on(0)
    zero = jnp.zeros((1,) + slab.shape[1:], slab.dtype)
    slab[pl.ds(0, 1)] = zero
    slab[pl.ds(slab.shape[0] - 1, 1)] = zero
    for k in range(1, nv):
        gather_copy(k).wait_recv()
        pass_on(k)
    for j in range(1, nv):
        owner = lax.rem(v + j, nv)
        pltpu.make_async_remote_copy(
            vol, spot(owner, s), s2.at[0], r2.at[j],
            device_id=(owner, f), device_id_type=MESH).wait_recv()
        for t in range(1, rep):
            side_copy(spot(owner, s), owner, j, t).start()
    pltpu.make_async_copy(vol, spot(v, s), own_sem).wait()
    load.wait()
    for j in range(nv):
        owner = lax.rem(v + j, nv)
        for t in range(1, rep):
            part = lax.rem(s - t + rep, rep)
            pltpu.make_async_remote_copy(
                vol, spot(owner, part), s3.at[t, j], r3.at[t, j],
                device_id=(v, q * rep + part), device_id_type=MESH).wait_recv()

    lane = lax.broadcasted_iota(jnp.int32, (filters, cells), 1)
    row = lane // W
    col = lane % W

    def shifted(x, step, keep):
        return jnp.where(keep, pltpu.roll(x, (-step) % cells, 1), 0.0)

    def convolve(block, dest):
        def step(i, carry):
            base = block * planes + 2 * i
            xs = [slab[base + a] for a in range(4)]
            cols = [jnp.concatenate([xs[a], xs[a + 1]], axis=1) for a in range(3)]
            if depth % 128 == 0:
                rhs = jnp.concatenate(cols, axis=0)
                for b in range(3):
                    lhs = jnp.concatenate(
                        [taps[a, pl.ds(3 * b, 3)].reshape(3 * filters, depth) for a in range(3)], axis=1)
                    prod[pl.ds(3 * b * filters, 3 * filters)] = jnp.dot(
                        lhs, rhs, preferred_element_type=jnp.float32)
            else:
                for b in range(3):
                    prod[pl.ds(3 * b * filters, 3 * filters)] = sum(
                        jnp.dot(taps[a, pl.ds(3 * b, 3)].reshape(3 * filters, depth), cols[a],
                                preferred_element_type=jnp.float32) for a in range(3))
            for side in range(2):
                total = None
                for b in range(3):
                    part = None
                    for e in range(3):
                        x = prod[pl.ds((3 * b + e) * filters, filters), pl.ds(side * cells, cells)]
                        if e != 1:
                            x = shifted(x, e - 1, (col + e >= 1) & (col + e <= W))
                        part = x if part is None else part + x
                    if b != 1:
                        part = shifted(part, (b - 1) * W, (row + b >= 1) & (row + b <= H))
                    total = part if total is None else total + part
                dest[2 * i + side] = total
            return carry
        lax.fori_loop(0, planes // 2, step, 0)

    def near_copy(m):
        return pltpu.make_async_remote_copy(
            away.at[m], near.at[m], s4.at[m], r4.at[m],
            device_id=(sibling, f), device_id_type=MESH)

    def far_copy(m):
        return pltpu.make_async_remote_copy(
            mine.at[m], far.at[m], s5.at[m], r5.at[m],
            device_id=(2 * lax.rem(pair + m, half) + core, f), device_id_type=MESH)

    for m in list(range(1, half)) + [0]:
        other = 2 * lax.rem(pair + m, half)
        convolve(other + 1 - core, away.at[m])
        near_copy(m).start()
        convolve(other + core, mine.at[m])
        near_copy(m).wait_recv()
        if m > 0:
            mine[m] = mine[m] + near[m]
            far_copy(m).start()
    total = mine[0] + near[0]
    for m in range(1, half):
        far_copy(m).wait_recv()
        total = total + far[m]
    out[...] = total

    for k in range(1, nv):
        gather_copy(k).wait_send()
    for k in range(nv):
        origin = lax.rem(q - k + nv, nv)

        @pl.when(origin != v)
        def _():
            cross_copy(vol, k, origin).wait_send()
    for j in range(nv):
        for t in range(1, rep):
            side_copy(vol, v, j, t).wait_send()
    for m in range(half):
        near_copy(m).wait_send()
        if m > 0:
            far_copy(m).wait_send()


def shards(nv, nf, volume, kernel, bias):
    rep = nf // nv
    chans, planes, cells = volume.shape
    filters, depth = kernel.shape[1:]
    half = nv // 2
    blocks = jnp.transpose(volume, (1, 0, 2))
    taps = kernel.reshape(3, 9, filters, depth)
    part = (half, planes, filters, cells)
    dma = pltpu.SemaphoreType.DMA
    total = pl.pallas_call(
        functools.partial(body, nv, rep),
        out_shape=jax.ShapeDtypeStruct((planes, filters, cells), jnp.float32),
        in_specs=[pl.BlockSpec(memory_space=pltpu.VMEM), pl.BlockSpec(memory_space=pl.ANY)],
        out_specs=pl.BlockSpec(memory_space=pltpu.VMEM),
        scratch_shapes=[
            pltpu.VMEM((nv, planes, chans, cells), jnp.bfloat16),
            pltpu.VMEM((nv * planes + 2, depth, cells), jnp.bfloat16),
            pltpu.VMEM((3, 9, filters, depth), jnp.bfloat16),
            pltpu.VMEM((9 * filters, 2 * cells), jnp.float32),
            pltpu.VMEM(part, jnp.float32),
            pltpu.VMEM(part, jnp.float32),
            pltpu.VMEM(part, jnp.float32),
            pltpu.VMEM(part, jnp.float32),
            dma, dma, dma((nv,)), dma((nv,)), dma((nv,)), dma((nv,)),
            dma((rep, nv)), dma((rep, nv)), dma((half,)), dma((half,)), dma((half,)), dma((half,)),
        ],
        compiler_params=pltpu.CompilerParams(
            collective_id=0, has_side_effects=True, vmem_limit_bytes=40 * 1024 * 1024),
        cost_estimate=pl.CostEstimate(
            flops=2 * 27 * filters * depth * nv * planes * cells,
            bytes_accessed=2 * 27 * filters * depth, transcendentals=0),
    )(blocks, taps)
    summed = jnp.transpose(total, (1, 0, 2)) + bias[:, None, None]
    return summed.astype(jnp.bfloat16)


def solution(mesh):
    in_specs = (P("filt", "vox", None), P(None, "filt", "vox"), P("filt"))
    out_specs = P("filt", "vox", None)
    work = functools.partial(shards, mesh.shape["vox"], mesh.shape["filt"])
    return jax.shard_map(work, mesh=mesh, in_specs=in_specs, out_specs=out_specs, check_vma=False)
```

```python
import functools

import jax
import jax.numpy as jnp
from jax import lax
from jax.experimental import pallas as pl
from jax.experimental.pallas import tpu as pltpu
from jax.sharding import PartitionSpec as P

H = 4
W = 32
CHUNKS = 2
MESH = pl.DeviceIdType.MESH


def body(
    nv, rep, vol, ker, out, held, slab, taps, prod, mine, away, near, far,
    tap_sem, own_sem, s1, r1, s2, r2, s3, r3, s4, r4, s5, r5,
):
    v = lax.axis_index("vox")
    f = lax.axis_index("filt")
    q = lax.div(f, rep)
    s = lax.rem(f, rep)
    planes, chans, cells = vol.shape
    filters = taps.shape[2]
    depth = taps.shape[3]
    half = nv // 2
    pair = lax.div(v, 2)
    core = lax.rem(v, 2)
    sibling = v + 1 - 2 * core

    load = pltpu.make_async_copy(ker, taps, tap_sem)
    load.start()

    def vox_at(dp, dc):
        return 2 * lax.rem(pair + dp, half) + lax.rem(core + dc, 2)

    offsets = [(dp, dc) for dp in range(half) for dc in range(2)]
    barrier = pltpu.get_barrier_semaphore()
    peers = [(v, lax.rem(q + k, nv) * rep + s) for k in (1, nv - 1)]
    peers += [(vox_at(dp, dc), f) for dp, dc in offsets[1:]]
    peers += [(v, q * rep + lax.rem(s + t, rep)) for t in range(1, rep)]
    for peer in peers:
        pl.semaphore_signal(barrier, inc=1, device_id=peer, device_id_type=MESH)
    pl.semaphore_wait(barrier, len(peers))

    size = planes // CHUNKS

    def spot(owner, part, piece):
        rows = pl.ds(pl.multiple_of(part * chans, chans), chans)
        return slab.at[pl.ds(1 + owner * planes + piece * size, size), rows, :]

    def own(piece):
        return vol.at[pl.ds(piece * size, size)]

    def hold(origin, piece):
        return held.at[origin, pl.ds(piece * size, size)]

    def line_copy(src, origin, piece, way):
        target = q + 1 if way == 0 else q - 1
        return pltpu.make_async_remote_copy(
            src, hold(origin, piece), s1.at[way, origin, piece], r1.at[origin, piece],
            device_id=(v, target * rep + s), device_id_type=MESH)

    def cross_copy(src, target, piece):
        place = 2 * lax.rem(pair - lax.div(target, 2) + half, half) + lax.rem(core + target, 2)
        return pltpu.make_async_remote_copy(
            src, spot(v, s, piece), s2.at[target, piece], r2.at[place, piece],
            device_id=(target, f), device_id_type=MESH)

    def side_copy(src, owner, place, piece, t):
        return pltpu.make_async_remote_copy(
            src, spot(owner, s, piece), s3.at[t, place, piece], r3.at[t, place, piece],
            device_id=(v, q * rep + lax.rem(s + t, rep)), device_id_type=MESH)

    first_dc = lax.rem(1 + pair + core, 2)
    owner_first = first_dc == 0

    def spread(src, origin, piece):
        @pl.when(origin == v)
        def _():
            @pl.when(owner_first)
            def _():
                for t in range(1, rep):
                    side_copy(src, v, 0, piece, t).start()
            pltpu.make_async_copy(src, spot(v, s, piece), own_sem.at[piece]).start()

        @pl.when(origin != v)
        def _():
            cross_copy(src, origin, piece).start()

    def own_wait(piece):
        pltpu.make_async_copy(own(piece), spot(v, s, piece), own_sem.at[piece]).wait()

    def pass_side(dp, dc, piece):
        place = 2 * dp + dc
        owner = vox_at(dp, dc)
        if place == 0:
            own_wait(piece)
        else:
            pltpu.make_async_remote_copy(
                own(piece), spot(owner, s, piece), s2.at[0, piece], r2.at[place, piece],
                device_id=(owner, f), device_id_type=MESH).wait_recv()
        for t in range(1, rep):
            side_copy(spot(owner, s, piece), owner, place, piece, t).start()

    def relay(piece):
        @pl.when(jnp.logical_not(owner_first))
        def _():
            pass_side(0, 1, piece)
        for dp, dc in offsets[2:]:
            pass_side(dp, dc, piece)

        if piece == CHUNKS - 1:
            for late in range(CHUNKS):
                @pl.when(owner_first)
                def _():
                    pass_side(0, 1, late)

                @pl.when(jnp.logical_not(owner_first))
                def _():
                    pass_side(0, 0, late)

    far_off = jnp.abs(v - q)
    for piece in range(CHUNKS):
        @pl.when(q < nv - 1)
        def _():
            line_copy(own(piece), q, piece, 0).start()

        @pl.when(q > 0)
        def _():
            line_copy(own(piece), q, piece, 1).start()

    for piece in range(CHUNKS):
        spread(own(piece), q, piece)
    zero = jnp.zeros((1,) + slab.shape[1:], slab.dtype)
    slab[pl.ds(0, 1)] = zero
    slab[pl.ds(slab.shape[0] - 1, 1)] = zero
    waiting = [(0, piece) for piece in range(CHUNKS)]
    for d in range(1, nv):
        for piece in range(CHUNKS):
            @pl.when(q >= d)
            def _():
                origin = q - d
                line_copy(own(piece), origin, piece, 0).wait_recv()

                @pl.when(q < nv - 1)
                def _():
                    line_copy(hold(origin, piece), origin, piece, 0).start()
                spread(hold(origin, piece), origin, piece)

            @pl.when(q + d < nv)
            def _():
                origin = q + d
                line_copy(own(piece), origin, piece, 1).wait_recv()

                @pl.when(q > 0)
                def _():
                    line_copy(hold(origin, piece), origin, piece, 1).start()
                spread(hold(origin, piece), origin, piece)

            waiting.append((d, piece))
            if len(waiting) > CHUNKS:
                first, late = waiting.pop(0)

                @pl.when(far_off == first)
                def _():
                    relay(late)

    for first, late in waiting:
        @pl.when(far_off == first)
        def _():
            relay(late)

    @pl.when(owner_first)
    def _():
        for piece in range(CHUNKS):
            own_wait(piece)
    load.wait()

    def arrived(dp, dc):
        owner = vox_at(dp, dc)
        place = 2 * dp + dc
        for piece in range(CHUNKS):
            for t in range(1, rep):
                part = lax.rem(s - t + rep, rep)
                pltpu.make_async_remote_copy(
                    own(piece), spot(owner, part, piece), s3.at[t, place, piece], r3.at[t, place, piece],
                    device_id=(v, q * rep + part), device_id_type=MESH).wait_recv()

    arrived(0, first_dc)
    for dp, dc in offsets[2:]:
        arrived(dp, dc)
    if half != 2:
        arrived(0, 1 - first_dc)

    lane = lax.broadcasted_iota(jnp.int32, (filters, cells), 1)
    row = lane // W
    col = lane % W

    def shifted(x, step, keep):
        return jnp.where(keep, pltpu.roll(x, (-step) % cells, 1), 0.0)

    def convolve(block, dest, i):
        base = block * planes + 2 * i
        xs = [slab[base + a] for a in range(4)]
        cols = [jnp.concatenate([xs[a], xs[a + 1]], axis=1) for a in range(3)]
        if depth % 128 == 0:
            rhs = jnp.concatenate(cols, axis=0)
            for b in range(3):
                lhs = jnp.concatenate(
                    [taps[a, pl.ds(3 * b, 3)].reshape(3 * filters, depth) for a in range(3)], axis=1)
                prod[pl.ds(3 * b * filters, 3 * filters)] = jnp.dot(
                    lhs, rhs, preferred_element_type=jnp.float32)
        else:
            for b in range(3):
                prod[pl.ds(3 * b * filters, 3 * filters)] = sum(
                    jnp.dot(taps[a, pl.ds(3 * b, 3)].reshape(3 * filters, depth), cols[a],
                            preferred_element_type=jnp.float32) for a in range(3))
        for side in range(2):
            total = None
            for b in range(3):
                part = None
                for e in range(3):
                    x = prod[pl.ds((3 * b + e) * filters, filters), pl.ds(side * cells, cells)]
                    if e != 1:
                        x = shifted(x, e - 1, (col + e >= 1) & (col + e <= W))
                    part = x if part is None else part + x
                if b != 1:
                    part = shifted(part, (b - 1) * W, (row + b >= 1) & (row + b <= H))
                total = part if total is None else total + part
            dest[2 * i + side] = total

    def near_copy(m, i):
        return pltpu.make_async_remote_copy(
            away.at[m, pl.ds(2 * i, 2)], near.at[m, pl.ds(2 * i, 2)], s4.at[m, i], r4.at[m, i],
            device_id=(sibling, f), device_id_type=MESH)

    def far_copy(m, i):
        return pltpu.make_async_remote_copy(
            mine.at[m, pl.ds(2 * i, 2)], far.at[m, pl.ds(2 * i, 2)], s5.at[m, i], r5.at[m, i],
            device_id=(2 * lax.rem(pair + m, half) + core, f), device_id_type=MESH)

    steps = planes // 2
    for m in list(range(1, half)) + [0]:
        other = 2 * lax.rem(pair + m, half)
        if m == 0 and half == 2:
            arrived(0, 1 - first_dc)

        def work(i, carry):
            rows = pl.ds(2 * i, 2)
            convolve(other + 1 - core, away.at[m], i)
            near_copy(m, i).start()
            convolve(other + core, mine.at[m], i)
            if m > 0:
                near_copy(m, i).wait_recv()
                mine[m, rows] = mine[m, rows] + near[m, rows]
                far_copy(m, i).start()
            return carry
        lax.fori_loop(0, steps, work, 0)
    for i in range(steps):
        rows = pl.ds(2 * i, 2)
        near_copy(0, i).wait_recv()
        total = mine[0, rows] + near[0, rows]
        for m in range(1, half):
            far_copy(m, i).wait_recv()
            total = total + far[m, rows]
        out[rows] = total

    for piece in range(CHUNKS):
        for origin in range(nv):
            @pl.when((origin <= q) & (q < nv - 1))
            def _():
                line_copy(own(piece), origin, piece, 0).wait_send()

            @pl.when((origin >= q) & (q > 0))
            def _():
                line_copy(own(piece), origin, piece, 1).wait_send()

            @pl.when(origin != v)
            def _():
                cross_copy(own(piece), origin, piece).wait_send()
        for place in range(nv):
            for t in range(1, rep):
                side_copy(own(piece), v, place, piece, t).wait_send()
    for m in range(half):
        for i in range(steps):
            near_copy(m, i).wait_send()
            if m > 0:
                far_copy(m, i).wait_send()


def shards(nv, nf, volume, kernel, bias):
    rep = nf // nv
    chans, planes, cells = volume.shape
    filters, depth = kernel.shape[1:]
    half = nv // 2
    steps = planes // 2
    blocks = jnp.transpose(volume, (1, 0, 2))
    taps = kernel.reshape(3, 9, filters, depth)
    part = (half, planes, filters, cells)
    dma = pltpu.SemaphoreType.DMA
    total = pl.pallas_call(
        functools.partial(body, nv, rep),
        out_shape=jax.ShapeDtypeStruct((planes, filters, cells), jnp.float32),
        in_specs=[pl.BlockSpec(memory_space=pltpu.VMEM), pl.BlockSpec(memory_space=pl.ANY)],
        out_specs=pl.BlockSpec(memory_space=pltpu.VMEM),
        scratch_shapes=[
            pltpu.VMEM((nv, planes, chans, cells), jnp.bfloat16),
            pltpu.VMEM((nv * planes + 2, depth, cells), jnp.bfloat16),
            pltpu.VMEM((3, 9, filters, depth), jnp.bfloat16),
            pltpu.VMEM((9 * filters, 2 * cells), jnp.float32),
            pltpu.VMEM(part, jnp.float32),
            pltpu.VMEM(part, jnp.float32),
            pltpu.VMEM(part, jnp.float32),
            pltpu.VMEM(part, jnp.float32),
            dma, dma((CHUNKS,)), dma((2, nv, CHUNKS)), dma((nv, CHUNKS)), dma((nv, CHUNKS)), dma((nv, CHUNKS)),
            dma((rep, nv, CHUNKS)), dma((rep, nv, CHUNKS)), dma((half, steps)), dma((half, steps)), dma((half, steps)), dma((half, steps)),
        ],
        compiler_params=pltpu.CompilerParams(
            collective_id=0, has_side_effects=True, vmem_limit_bytes=60 * 1024 * 1024),
        cost_estimate=pl.CostEstimate(
            flops=2 * 27 * filters * depth * nv * planes * cells,
            bytes_accessed=2 * 27 * filters * depth, transcendentals=0),
    )(blocks, taps)
    summed = jnp.transpose(total, (1, 0, 2)) + bias[:, None, None]
    return summed.astype(jnp.bfloat16)


def solution(mesh):
    in_specs = (P("filt", "vox", None), P(None, "filt", "vox"), P("filt"))
    out_specs = P("filt", "vox", None)
    work = functools.partial(shards, mesh.shape["vox"], mesh.shape["filt"])
    return jax.shard_map(work, mesh=mesh, in_specs=in_specs, out_specs=out_specs, check_vma=False)
```

```python
import functools

import jax
import jax.numpy as jnp
from jax import lax
from jax.experimental import pallas as pl
from jax.experimental.pallas import tpu as pltpu
from jax.sharding import PartitionSpec as P

H = 4
W = 32
CHUNKS = 2
MESH = pl.DeviceIdType.MESH


def body(
    nv, rep, vol, ker, out, held, slab, taps, prod, mine, away, near, far,
    tap_sem, own_sem, s1, r1, s2, r2, s3, r3, s4, r4, s5, r5,
):
    v = lax.axis_index("vox")
    f = lax.axis_index("filt")
    q = lax.div(f, rep)
    s = lax.rem(f, rep)
    planes, chans, cells = vol.shape
    filters = taps.shape[2]
    depth = taps.shape[3]
    half = nv // 2
    pair = lax.div(v, 2)
    core = lax.rem(v, 2)
    sibling = v + 1 - 2 * core

    load = pltpu.make_async_copy(ker, taps, tap_sem)
    load.start()

    def vox_at(dp, dc):
        return 2 * lax.rem(pair + dp, half) + lax.rem(core + dc, 2)

    offsets = [(dp, dc) for dp in range(half) for dc in range(2)]
    barrier = pltpu.get_barrier_semaphore()
    peers = [(v, lax.rem(q + k, nv) * rep + s) for k in (1, nv - 1)]
    peers += [(vox_at(dp, dc), f) for dp, dc in offsets[1:]]
    peers += [(v, q * rep + lax.rem(s + t, rep)) for t in range(1, rep)]
    for peer in peers:
        pl.semaphore_signal(barrier, inc=1, device_id=peer, device_id_type=MESH)
    pl.semaphore_wait(barrier, len(peers))

    size = planes // CHUNKS

    def spot(owner, part, piece):
        rows = pl.ds(pl.multiple_of(part * chans, chans), chans)
        return slab.at[pl.ds(1 + owner * planes + piece * size, size), rows, :]

    def own(piece):
        return vol.at[pl.ds(piece * size, size)]

    def hold(origin, piece):
        return held.at[origin, pl.ds(piece * size, size)]

    def line_copy(src, origin, piece, way):
        target = q + 1 if way == 0 else q - 1
        return pltpu.make_async_remote_copy(
            src, hold(origin, piece), s1.at[way, origin, piece], r1.at[origin, piece],
            device_id=(v, target * rep + s), device_id_type=MESH)

    def cross_copy(src, target, piece):
        place = 2 * lax.rem(pair - lax.div(target, 2) + half, half) + lax.rem(core + target, 2)
        return pltpu.make_async_remote_copy(
            src, spot(v, s, piece), s2.at[target, piece], r2.at[place, piece],
            device_id=(target, f), device_id_type=MESH)

    def side_copy(src, owner, place, piece, t):
        return pltpu.make_async_remote_copy(
            src, spot(owner, s, piece), s3.at[t, place, piece], r3.at[t, place, piece],
            device_id=(v, q * rep + lax.rem(s + t, rep)), device_id_type=MESH)

    first_dc = lax.rem(1 + pair + core, 2)
    owner_first = first_dc == 0

    def spread(src, origin, piece):
        @pl.when(origin == v)
        def _():
            @pl.when(owner_first)
            def _():
                for t in range(1, rep):
                    side_copy(src, v, 0, piece, t).start()
            pltpu.make_async_copy(src, spot(v, s, piece), own_sem.at[piece]).start()

        @pl.when(origin != v)
        def _():
            cross_copy(src, origin, piece).start()

    def own_wait(piece):
        pltpu.make_async_copy(own(piece), spot(v, s, piece), own_sem.at[piece]).wait()

    def pass_side(dp, dc, piece):
        place = 2 * dp + dc
        owner = vox_at(dp, dc)
        if place == 0:
            own_wait(piece)
        else:
            pltpu.make_async_remote_copy(
                own(piece), spot(owner, s, piece), s2.at[0, piece], r2.at[place, piece],
                device_id=(owner, f), device_id_type=MESH).wait_recv()
        for t in range(1, rep):
            side_copy(spot(owner, s, piece), owner, place, piece, t).start()

    def relay(piece):
        @pl.when(jnp.logical_not(owner_first))
        def _():
            pass_side(0, 1, piece)
        for dp, dc in offsets[2:]:
            pass_side(dp, dc, piece)

        if piece == CHUNKS - 1:
            for late in range(CHUNKS):
                @pl.when(owner_first)
                def _():
                    pass_side(0, 1, late)

                @pl.when(jnp.logical_not(owner_first))
                def _():
                    pass_side(0, 0, late)

    far_off = jnp.abs(v - q)
    for piece in range(CHUNKS):
        @pl.when(q < nv - 1)
        def _():
            line_copy(own(piece), q, piece, 0).start()

        @pl.when(q > 0)
        def _():
            line_copy(own(piece), q, piece, 1).start()

    for piece in range(CHUNKS):
        spread(own(piece), q, piece)
    zero = jnp.zeros((1,) + slab.shape[1:], slab.dtype)
    slab[pl.ds(0, 1)] = zero
    slab[pl.ds(slab.shape[0] - 1, 1)] = zero
    waiting = [(0, piece) for piece in range(CHUNKS)]
    for d in range(1, nv):
        for piece in range(CHUNKS):
            @pl.when(q >= d)
            def _():
                origin = q - d
                line_copy(own(piece), origin, piece, 0).wait_recv()

                @pl.when(q < nv - 1)
                def _():
                    line_copy(hold(origin, piece), origin, piece, 0).start()
                spread(hold(origin, piece), origin, piece)

            @pl.when(q + d < nv)
            def _():
                origin = q + d
                line_copy(own(piece), origin, piece, 1).wait_recv()

                @pl.when(q > 0)
                def _():
                    line_copy(hold(origin, piece), origin, piece, 1).start()
                spread(hold(origin, piece), origin, piece)

            waiting.append((d, piece))
            if len(waiting) > CHUNKS:
                first, late = waiting.pop(0)

                @pl.when(far_off == first)
                def _():
                    relay(late)

    for first, late in waiting:
        @pl.when(far_off == first)
        def _():
            relay(late)

    @pl.when(owner_first)
    def _():
        for piece in range(CHUNKS):
            own_wait(piece)
    load.wait()

    def arrived(dp, dc):
        owner = vox_at(dp, dc)
        place = 2 * dp + dc
        for piece in range(CHUNKS):
            for t in range(1, rep):
                part = lax.rem(s - t + rep, rep)
                pltpu.make_async_remote_copy(
                    own(piece), spot(owner, part, piece), s3.at[t, place, piece], r3.at[t, place, piece],
                    device_id=(v, q * rep + part), device_id_type=MESH).wait_recv()

    arrived(0, first_dc)
    for dp, dc in offsets[2:]:
        arrived(dp, dc)
    if half != 2:
        arrived(0, 1 - first_dc)

    lane = lax.broadcasted_iota(jnp.int32, (filters, cells), 1)
    row = lane // W
    col = lane % W

    def shifted(x, step, keep):
        return jnp.where(keep, pltpu.roll(x, (-step) % cells, 1), 0.0)

    def convolve(block, dest, i):
        base = block * planes + 2 * i
        xs = [slab[base + a] for a in range(4)]
        cols = [jnp.concatenate([xs[a], xs[a + 1]], axis=1) for a in range(3)]
        if depth % 128 == 0:
            rhs = jnp.concatenate(cols, axis=0)
            for b in range(3):
                lhs = jnp.concatenate(
                    [taps[a, pl.ds(3 * b, 3)].reshape(3 * filters, depth) for a in range(3)], axis=1)
                prod[pl.ds(3 * b * filters, 3 * filters)] = jnp.dot(
                    lhs, rhs, preferred_element_type=jnp.float32)
        else:
            for b in range(3):
                prod[pl.ds(3 * b * filters, 3 * filters)] = sum(
                    jnp.dot(taps[a, pl.ds(3 * b, 3)].reshape(3 * filters, depth), cols[a],
                            preferred_element_type=jnp.float32) for a in range(3))
        for side in range(2):
            total = None
            for b in range(3):
                part = None
                for e in range(3):
                    x = prod[pl.ds((3 * b + e) * filters, filters), pl.ds(side * cells, cells)]
                    if e != 1:
                        x = shifted(x, e - 1, (col + e >= 1) & (col + e <= W))
                    part = x if part is None else part + x
                if b != 1:
                    part = shifted(part, (b - 1) * W, (row + b >= 1) & (row + b <= H))
                total = part if total is None else total + part
            dest[2 * i + side] = total

    def near_copy(m, i):
        return pltpu.make_async_remote_copy(
            away.at[m, pl.ds(2 * i, 2)], near.at[m, pl.ds(2 * i, 2)], s4.at[m, i], r4.at[m, i],
            device_id=(sibling, f), device_id_type=MESH)

    def far_copy(m, i):
        return pltpu.make_async_remote_copy(
            mine.at[m, pl.ds(2 * i, 2)], far.at[m, pl.ds(2 * i, 2)], s5.at[m, i], r5.at[m, i],
            device_id=(2 * lax.rem(pair + m, half) + core, f), device_id_type=MESH)

    steps = planes // 2
    for m in list(range(1, half)) + [0]:
        other = 2 * lax.rem(pair + m, half)
        if m == 0 and half == 2:
            arrived(0, 1 - first_dc)

        def work(i, carry):
            rows = pl.ds(2 * i, 2)
            convolve(other + 1 - core, away.at[m], i)
            near_copy(m, i).start()
            convolve(other + core, mine.at[m], i)
            if m > 0:
                near_copy(m, i).wait_recv()
                mine[m, rows] = mine[m, rows] + near[m, rows]
                far_copy(m, i).start()
            return carry
        lax.fori_loop(0, steps, work, 0)
    for i in range(steps):
        rows = pl.ds(2 * i, 2)
        near_copy(0, i).wait_recv()
        total = mine[0, rows] + near[0, rows]
        for m in range(1, half):
            far_copy(m, i).wait_recv()
            total = total + far[m, rows]
        out[rows] = total

    for piece in range(CHUNKS):
        for origin in range(nv):
            @pl.when((origin <= q) & (q < nv - 1))
            def _():
                line_copy(own(piece), origin, piece, 0).wait_send()

            @pl.when((origin >= q) & (q > 0))
            def _():
                line_copy(own(piece), origin, piece, 1).wait_send()

            @pl.when(origin != v)
            def _():
                cross_copy(own(piece), origin, piece).wait_send()
        for place in range(nv):
            for t in range(1, rep):
                side_copy(own(piece), v, place, piece, t).wait_send()
    for m in range(half):
        for i in range(steps):
            near_copy(m, i).wait_send()
            if m > 0:
                far_copy(m, i).wait_send()


def shards(nv, nf, volume, kernel, bias):
    rep = nf // nv
    chans, planes, cells = volume.shape
    filters, depth = kernel.shape[1:]
    half = nv // 2
    steps = planes // 2
    blocks = jnp.transpose(volume, (1, 0, 2))
    taps = kernel.reshape(3, 9, filters, depth)
    part = (half, planes, filters, cells)
    dma = pltpu.SemaphoreType.DMA
    total = pl.pallas_call(
        functools.partial(body, nv, rep),
        out_shape=jax.ShapeDtypeStruct((planes, filters, cells), jnp.float32),
        in_specs=[pl.BlockSpec(memory_space=pltpu.VMEM), pl.BlockSpec(memory_space=pl.ANY)],
        out_specs=pl.BlockSpec(memory_space=pltpu.VMEM),
        scratch_shapes=[
            pltpu.VMEM((nv, planes, chans, cells), jnp.bfloat16),
            pltpu.VMEM((nv * planes + 2, depth, cells), jnp.bfloat16),
            pltpu.VMEM((3, 9, filters, depth), jnp.bfloat16),
            pltpu.VMEM((9 * filters, 2 * cells), jnp.float32),
            pltpu.VMEM(part, jnp.float32),
            pltpu.VMEM(part, jnp.float32),
            pltpu.VMEM(part, jnp.float32),
            pltpu.VMEM(part, jnp.float32),
            dma, dma((CHUNKS,)), dma((2, nv, CHUNKS)), dma((nv, CHUNKS)), dma((nv, CHUNKS)), dma((nv, CHUNKS)),
            dma((rep, nv, CHUNKS)), dma((rep, nv, CHUNKS)), dma((half, steps)), dma((half, steps)), dma((half, steps)), dma((half, steps)),
        ],
        compiler_params=pltpu.CompilerParams(
            collective_id=0, has_side_effects=True, vmem_limit_bytes=53 * 1024 * 1024),
        cost_estimate=pl.CostEstimate(
            flops=2 * 27 * filters * depth * nv * planes * cells,
            bytes_accessed=2 * 27 * filters * depth, transcendentals=0),
    )(blocks, taps)
    summed = jnp.transpose(total, (1, 0, 2)) + bias[:, None, None]
    return summed.astype(jnp.bfloat16)


def solution(mesh):
    in_specs = (P("filt", "vox", None), P(None, "filt", "vox"), P("filt"))
    out_specs = P("filt", "vox", None)
    work = functools.partial(shards, mesh.shape["vox"], mesh.shape["filt"])
    return jax.shard_map(work, mesh=mesh, in_specs=in_specs, out_specs=out_specs, check_vma=False)
```
